256 devices in a mesh: rows: 32 (over z_hi, y, core), cols: 8 (over x, z_lo).
Axes of the slice: x: 4, y: 4, z: 8 (z_hi: 4, z_lo: 2; z = z_hi * 2 + z_lo), core: 2. Of those that a mesh axis runs over, the one named last changes fastest.
Arguments:
- queries: bfloat16 [1024, 16384], P(None, 'rows'), may hold values from -6 to 6
- inverse_gram: bfloat16 [16384, 16384], P('rows', 'cols'), may hold values from -2 to 2, as said below
- slab: bfloat16 [8192, 16384], P('rows', 'cols'), may hold values from -0.046875 to 0.046875
Outputs:
- scores: bfloat16 [1024, 8192], P('cols', 'rows')
The draws below stay inside these ranges and needn't reach their ends.
Inputs may be any that keep to these rules, and one draw needn't show every extreme that they name: inverse_gram has a diagonal of 0.5 to 2 and small entries elsewhere.
All inputs are finite; a program needn't handle non-finite values.
Results may differ from the reference program's by a relative error of at most 0.0049.
Values may be sent and summed in bfloat16 or wider, within the bound.
No kernel may reach another device: no remote copies, remote signals or barrier semaphores. Data moves between devices by JAX's collectives and lax.ppermute only.
A program may use at most 64 MiB of HBM per device.

```python
import math
import jax
import jax.numpy as jnp
from jax import lax

P_SIZE = 16384
NQ = 1024
M = 8192


def draw_inverse_gram(key, part):
    key = jax.random.fold_in(key, 7)
    noise_key = jax.random.fold_in(key, 1)
    diag_key = jax.random.fold_in(key, 2)
    noise = jax.random.truncated_normal(noise_key, -6.0, 6.0, (P_SIZE, P_SIZE), jnp.float32)
    off = noise * (0.7 / math.sqrt(P_SIZE))
    diag = jax.random.uniform(diag_key, (P_SIZE,), jnp.float32, 0.5, 2.0)
    left = lax.broadcasted_iota(jnp.int32, (P_SIZE, P_SIZE), 0)
    right = lax.broadcasted_iota(jnp.int32, (P_SIZE, P_SIZE), 1)
    whole = jnp.where(left == right, diag[:, None], off)
    return whole.astype(jnp.bfloat16)


def raised(array, key, source, target, blocks, factor):
    owner, partner = [(jnp.arange(array.shape[axis_at]) // (array.shape[axis_at] // blocks)).reshape([-1 if axis == axis_at else 1 for axis in range(array.ndim)]) for axis_at in (source, target)]
    chosen = jax.random.permutation(key, blocks)[partner]
    strong = (owner == chosen) | (owner == (partner + blocks // 2) % blocks)
    return jnp.where(strong, factor * array, array)


def block_scale(stream_key, dims, shards, low, top_value):
    def one(axis_at, blocks):
        steps = jax.random.uniform(jax.random.fold_in(jax.random.fold_in(stream_key, 6), axis_at), (blocks,), jnp.float32, low / len(shards), top_value / len(shards))
        return jnp.repeat(jnp.exp(steps), dims[axis_at] // blocks).reshape((-1,) + (1,) * (len(dims) - axis_at - 1))

    gain = one(*shards[0])
    for cut in shards[1:]:
        gain = gain * one(*cut)
    return gain


def gaussian(own_key, shape, spread, bound, pieces=(), held_as=jnp.bfloat16):
    values = jax.random.normal(own_key, shape, jnp.float32) * spread
    if len(pieces) > 0:
        values = block_scale(own_key, shape, pieces, -0.22, 0.18) * values
    return jnp.clip(values, min=-bound, max=bound).astype(held_as)


def gaussian_with(key, shape, scale, most, cuts, heavy, kind=jnp.bfloat16):
    values = scale * jax.random.normal(key, shape, jnp.float32)
    if cuts:
        values = values * block_scale(key, shape, cuts, -0.22, 0.18)
    return jnp.clip(raised(values, jax.random.fold_in(key, 3), *heavy), -most, most).astype(kind)


def setup_inputs(seed: int = 0) -> dict:
    key_of = jax.random.split(jax.random.key(seed), 4)
    return {
        "queries": gaussian_with(key_of[0], (NQ, P_SIZE), 1.0, 6.0, ((1, 32),), (1, 0, 32, 2.75)),
        "inverse_gram": draw_inverse_gram(jax.random.fold_in(key_of[3], 71), 0),
        "slab": gaussian(key_of[2], (M, P_SIZE), P_SIZE ** -0.5, 0.046875, ((0, 32), (1, 8))),
    }


def reference(queries, inverse_gram, slab):
    images = jnp.dot(queries, inverse_gram, preferred_element_type=jnp.float32).astype(jnp.bfloat16)
    scores = lax.dot_general(images, slab, (((1,), (1,)), ((), ())), preferred_element_type=jnp.float32)
    return scores.astype(jnp.bfloat16)
```

```python
import jax
import jax.numpy as jnp
from jax import lax
from jax.sharding import Mesh, PartitionSpec as P

F32, BF16 = jnp.float32, jnp.bfloat16
SWAP = [(0, 1), (1, 0)]
NEAR = [(0, 1), (1, 0), (2, 3), (3, 2)]
WRAP = [(0, 3), (3, 0), (1, 2), (2, 1)]


def shift(d):
    return [(i, (i + d) % 4) for i in range(4)]


def rolled(a, start):
    return lax.dynamic_slice_in_dim(jnp.concatenate([a, a]), start, a.shape[0], 0)


def dot(a, b):
    return jnp.dot(a, b, preferred_element_type=F32)


def columns(a, first):
    return lax.dynamic_slice_in_dim(a, first, 128, 1)


def local(queries, gram, slab, chunks=1):
    zh, y, k, x, zl = (lax.axis_index(n) for n in ("zh", "y", "core", "x", "zl"))
    a1, a2 = ((y + 1) // 2) % 2, y // 2
    b1, b2 = y // 2, y % 2
    order = []
    for half, (p, s, flip) in enumerate(((a1, b1, 0), (a2, b2, 1))):
        for part in (0, 1):
            first = 1 - s if part and flip else s
            for sub in (first, 1 - first):
                order.append(half * 4 + (1 - p if part else p) * 2 + sub)

    def half(a, core):
        return jnp.concatenate([columns(a, core * 1024 + o * 128) for o in order], axis=1)

    rows = rolled(queries.reshape(4, 2, 4, 32, 512), x)
    rows = rolled(rows.transpose(1, 0, 2, 3, 4), zl)
    rows = rolled(rows.transpose(2, 1, 0, 3, 4), zh)
    g_mine, g_other = half(gram, k), half(gram, 1 - k)
    s_mine, s_other = half(slab, k), half(slab, 1 - k)
    g_in = lax.ppermute(g_other, "core", SWAP)
    n = 32 // chunks
    outs = []
    q_in = lax.ppermute(rows, "core", SWAP)
    s_in = lax.ppermute(s_other, "core", SWAP)
    for c in range(chunks):
        q0 = rows[:, :, :, c * n:(c + 1) * n].reshape(32 * n, 512)
        q1 = q_in[:, :, :, c * n:(c + 1) * n].reshape(32 * n, 512)

        def part(lo, hi):
            return dot(q0, g_mine[:, lo:hi]) + dot(q1, g_in[:, lo:hi])

        got_a = lax.ppermute(part(256, 512).astype(BF16), "y", NEAR)
        got_b = lax.ppermute(part(768, 1024).astype(BF16), "y", WRAP)
        keep_a, keep_b = part(0, 256), part(512, 768)
        sum_a, sum_b = keep_a + got_a.astype(F32), keep_b + got_b.astype(F32)
        got_a = lax.ppermute(sum_a[:, 128:].astype(BF16), "y", WRAP)
        got_b = lax.ppermute(sum_b[:, 128:].astype(BF16), "y", NEAR)
        piece = jnp.concatenate([sum_a[:, :128] + got_a.astype(F32), sum_b[:, :128] + got_b.astype(F32)], axis=1)
        piece = piece.reshape(4, 8 * n, 256)
        own = piece[0]
        for d in (1, 2, 3):
            own = own + lax.ppermute(piece[d].astype(BF16), "zh", shift(d)).astype(F32)
        own = own.astype(BF16)
        z = jnp.concatenate([own] + [lax.ppermute(own, "zh", shift(-d)) for d in (1, 2, 3)], axis=0)
        za, zb = z[:, :128], z[:, 128:]
        aa = jnp.concatenate([za, lax.ppermute(za, "y", WRAP)], axis=1)
        bb = jnp.concatenate([zb, lax.ppermute(zb, "y", NEAR)], axis=1)
        images = jnp.concatenate([aa, lax.ppermute(aa, "y", NEAR), bb, lax.ppermute(bb, "y", WRAP)], axis=1)

        def scores(s):
            return lax.dot_general(images, s, (((1,), (1,)), ((), ())), preferred_element_type=F32)

        mine, other = scores(s_mine), scores(s_in)
        sc = mine + lax.ppermute(other, "core", SWAP)
        sc = sc.reshape(4, 4, 2, n, 256).transpose(1, 2, 0, 3, 4)
        own = sc[0]
        for d in (1, 2, 3):
            own = own + lax.ppermute(sc[d].astype(BF16), "x", shift(d)).astype(F32)
        own = own[0] + lax.ppermute(own[1].astype(BF16), "zl", SWAP).astype(F32)
        outs.append(own.astype(BF16))
    out = jnp.stack(outs, axis=1)
    out = rolled(out, (4 - zh) % 4)
    return out.reshape(128, 256)


def solution(mesh):
    fine = Mesh(mesh.devices.reshape(4, 4, 2, 4, 2), ("zh", "y", "core", "x", "zl"))
    rows, cols = ("zh", "y", "core"), ("x", "zl")
    return jax.shard_map(
        local,
        mesh=fine,
        in_specs=(P(None, rows), P(rows, cols), P(rows, cols)),
        out_specs=P(cols, rows),
        check_vma=False,
    )
```

```python
import jax
import jax.numpy as jnp
from jax import lax
from jax.sharding import Mesh, PartitionSpec as P

F32, BF16 = jnp.float32, jnp.bfloat16
AXES = ("zh", "y", "core", "x", "zl")
CHUNKS = 2
SWAP = [(0, 1), (1, 0)]
NEAR = [(0, 1), (1, 0), (2, 3), (3, 2)]
WRAP = [(0, 3), (3, 0), (1, 2), (2, 1)]


def by_core(first, second):
    return [(2 * s, 2 * d) for s, d in first] + [(2 * s + 1, 2 * d + 1) for s, d in second]


STEP1, STEP2 = by_core(NEAR, WRAP), by_core(WRAP, NEAR)


def dot(a, b):
    return jnp.dot(a, b, preferred_element_type=F32)


def dot_t(a, b):
    return lax.dot_general(a, b, (((1,), (1,)), ((), ())), preferred_element_type=F32)


def cut(a, i, size):
    return lax.dynamic_slice_in_dim(a, i * size, size, 1)


def local(queries, gram, slab):
    y, k = lax.axis_index("y"), lax.axis_index("core")
    p = jnp.where(k == 0, ((y + 1) // 2) % 2, y // 2)
    s = jnp.where(k == 0, y // 2, y % 2)
    t = jnp.where(k == 0, s, 1 - s)
    n = 512 // CHUNKS
    r = 64 // CHUNKS

    g_in = lax.ppermute(gram, "core", SWAP)
    rows = queries.reshape(8, 2, CHUNKS, r, 512)

    def for_core(core):
        picked = lax.dynamic_index_in_dim(rows, core, 1, keepdims=False)
        return picked.transpose(1, 0, 2, 3).reshape(CHUNKS, n, 512)

    q_mine = for_core(k)
    q_in = lax.ppermute(for_core(1 - k), "core", SWAP)
    s_in = lax.ppermute(slab, "core", SWAP)
    both = jnp.where(k == 0, jnp.concatenate([slab, s_in]), jnp.concatenate([s_in, slab]))
    s_cut = [cut(both, i, 512) for i in (2 * p + s, 2 * p + 1 - s, 2 * (1 - p) + t, 2 * (1 - p) + 1 - t)]
    outs = []
    for c in range(CHUNKS):
        part = dot(q_mine[c], gram) + dot(q_in[c], g_in)
        got = lax.ppermute(cut(part, 1 - p, 1024).astype(BF16), ("y", "core"), STEP1)
        part = cut(part, p, 1024) + got.astype(F32)
        got = lax.ppermute(cut(part, 1 - s, 512).astype(BF16), ("y", "core"), STEP2)
        piece = cut(part, s, 512) + got.astype(F32)
        piece = piece + lax.ppermute(piece.astype(BF16), ("zh", "core"), STEP1).astype(F32)
        piece = piece + lax.ppermute(piece.astype(BF16), ("zh", "core"), STEP2).astype(F32)
        i0 = piece.astype(BF16)
        i1 = lax.ppermute(i0, ("y", "core"), STEP2)
        i23 = lax.ppermute(jnp.concatenate([i0, i1], axis=1), ("y", "core"), STEP1)
        images = (i0, i1, i23[:, :512], i23[:, 512:])
        sc = sum(dot_t(i, b) for i, b in zip(images, s_cut))
        sc = sc.astype(BF16).reshape(8, r, 2, 256).transpose(2, 0, 1, 3).reshape(16, r, 256)
        sc = lax.all_to_all(sc, ("core", "x", "zl"), 0, 0, tiled=True)
        outs.append(sc.reshape(2, 8, r, 256).astype(F32).sum(axis=1).astype(BF16))
    return jnp.stack(outs, axis=1).reshape(128, 256)


def solution(mesh):
    fine = Mesh(mesh.devices.reshape(4, 4, 2, 4, 2), AXES)
    rows, cols = ("zh", "y", "core"), ("x", "zl")
    return jax.shard_map(
        local,
        mesh=fine,
        in_specs=(P(None, rows), P(rows, cols), P(rows, cols)),
        out_specs=P(cols, rows),
        check_vma=False,
    )
```

```python
import jax
import jax.numpy as jnp
from jax import lax
from jax.sharding import Mesh, PartitionSpec as P

F32, BF16 = jnp.float32, jnp.bfloat16
AXES = ("zh", "y", "core", "x", "zl")
CHUNKS = 2
SWAP = [(0, 1), (1, 0)]
NEAR = [(0, 1), (1, 0), (2, 3), (3, 2)]
WRAP = [(0, 3), (3, 0), (1, 2), (2, 1)]


def by_core(first, second):
    return [(2 * s, 2 * d) for s, d in first] + [(2 * s + 1, 2 * d + 1) for s, d in second]


STEP1, STEP2 = by_core(NEAR, WRAP), by_core(WRAP, NEAR)


def dot(a, b):
    return jnp.dot(a, b, preferred_element_type=F32)


def dot_t(a, b):
    return lax.dot_general(a, b, (((1,), (1,)), ((), ())), preferred_element_type=F32)


def cut(a, i, size):
    return lax.dynamic_slice_in_dim(a, i * size, size, 1)


def local(queries, gram, slab):
    y, k = lax.axis_index("y"), lax.axis_index("core")
    p = jnp.where(k == 0, ((y + 1) // 2) % 2, y // 2)
    s = jnp.where(k == 0, y // 2, y % 2)
    n = 512 // CHUNKS
    r = 64 // CHUNKS

    g_in = lax.ppermute(gram, "core", SWAP)
    rows = queries.reshape(8, 2, CHUNKS, r, 512)

    def for_core(core):
        picked = lax.dynamic_index_in_dim(rows, core, 1, keepdims=False)
        return picked.transpose(1, 0, 2, 3).reshape(CHUNKS, n, 512)

    q_mine = for_core(k)
    q_in = lax.ppermute(for_core(1 - k), "core", SWAP)
    s_in = lax.ppermute(slab, "core", SWAP)
    both = jnp.where(k == 0, jnp.concatenate([slab, s_in]), jnp.concatenate([s_in, slab]))
    s_kept, s_other = cut(both, p, 1024), cut(both, 1 - p, 1024)
    outs = []
    for c in range(CHUNKS):
        part = dot(q_mine[c], gram) + dot(q_in[c], g_in)
        got = lax.ppermute(cut(part, 1 - p, 1024).astype(BF16), ("y", "core"), STEP1)
        part = cut(part, p, 1024) + got.astype(F32)
        second = cut(part, 1 - s, 512).astype(BF16)
        got = lax.ppermute(second, ("y", "core"), STEP2)
        piece = cut(part, s, 512) + got.astype(F32)
        piece = piece + lax.ppermute(piece.astype(BF16), ("zh", "core"), STEP1).astype(F32)
        piece = piece + lax.ppermute(piece.astype(BF16), ("zh", "core"), STEP2).astype(F32)
        i0 = piece.astype(BF16)
        i1 = lax.ppermute(i0, ("y", "core"), STEP2)
        kept = jnp.where(s == 0, jnp.concatenate([i0, i1], axis=1), jnp.concatenate([i1, i0], axis=1))
        other = lax.ppermute(kept, ("y", "core"), STEP1)
        sc = dot_t(kept, s_kept) + dot_t(other, s_other)
        outs.append(sc.astype(BF16).reshape(8, r, 2, 256).transpose(2, 0, 1, 3))
    sc = jnp.stack(outs, axis=2).reshape(16, 64, 256)
    sc = lax.all_to_all(sc, ("core", "x", "zl"), 0, 0, tiled=True)
    return sc.reshape(2, 8, 64, 256).astype(F32).sum(axis=1).astype(BF16).reshape(128, 256)


def solution(mesh):
    fine = Mesh(mesh.devices.reshape(4, 4, 2, 4, 2), AXES)
    rows, cols = ("zh", "y", "core"), ("x", "zl")
    return jax.shard_map(
        local,
        mesh=fine,
        in_specs=(P(None, rows), P(rows, cols), P(rows, cols)),
        out_specs=P(cols, rows),
        check_vma=False,
    )
```

```python
import jax
import jax.numpy as jnp
from jax import lax
from jax.sharding import Mesh, PartitionSpec as P

F32, BF16 = jnp.float32, jnp.bfloat16
AXES = ("zh", "y", "core", "x", "zl")
CHUNKS = 2
SWAP = [(0, 1), (1, 0)]
NEAR = [(0, 1), (1, 0), (2, 3), (3, 2)]
WRAP = [(0, 3), (3, 0), (1, 2), (2, 1)]


def by_core(first, second):
    return [(2 * s, 2 * d) for s, d in first] + [(2 * s + 1, 2 * d + 1) for s, d in second]


STEP1, STEP2 = by_core(NEAR, WRAP), by_core(WRAP, NEAR)


def dot(a, b):
    return jnp.dot(a, b, preferred_element_type=F32)


def dot_t(a, b):
    return lax.dot_general(a, b, (((1,), (1,)), ((), ())), preferred_element_type=F32)


def cut(a, i, size):
    return lax.dynamic_slice_in_dim(a, i * size, size, 1)


def local(queries, gram, slab):
    y, k = lax.axis_index("y"), lax.axis_index("core")
    p = jnp.where(k == 0, ((y + 1) // 2) % 2, y // 2)
    s = jnp.where(k == 0, y // 2, y % 2)
    t = jnp.where(k == 0, s, 1 - s)
    n = 512 // CHUNKS
    r = 64 // CHUNKS

    g_in = lax.ppermute(gram, "core", SWAP)
    rows = queries.reshape(8, 2, CHUNKS, r, 512)

    def for_core(core):
        picked = lax.dynamic_index_in_dim(rows, core, 1, keepdims=False)
        return picked.transpose(1, 0, 2, 3).reshape(CHUNKS, n, 512)

    q_mine = for_core(k)
    q_in = lax.ppermute(for_core(1 - k), "core", SWAP)
    s_in = lax.ppermute(slab, "core", SWAP)
    both = jnp.concatenate([slab, s_in])
    s_kept = cut(both, p, 1024)
    s_second, s_third = cut(both, 2 * (1 - p) + t, 512), cut(both, 2 * (1 - p) + 1 - t, 512)
    outs = []
    for c in range(CHUNKS):
        part = dot(q_mine[c], gram) + dot(q_in[c], g_in)
        got = lax.ppermute(cut(part, 1 - p, 1024).astype(BF16), ("y", "core"), STEP1)
        part = cut(part, p, 1024) + got.astype(F32)
        second = cut(part, 1 - s, 512).astype(BF16)
        got = lax.ppermute(second, ("y", "core"), STEP2)
        piece = cut(part, s, 512) + got.astype(F32)
        piece = piece + lax.ppermute(piece.astype(BF16), ("zh", "core"), STEP1).astype(F32)
        piece = piece + lax.ppermute(piece.astype(BF16), ("zh", "core"), STEP2).astype(F32)
        i0 = piece.astype(BF16)
        i1 = lax.ppermute(i0, ("y", "core"), STEP2)
        kept = jnp.where(s == 0, jnp.concatenate([i0, i1], axis=1), jnp.concatenate([i1, i0], axis=1))
        i2 = lax.ppermute(i0, ("y", "core"), STEP1)
        i3 = lax.ppermute(i1, ("y", "core"), STEP1)
        sc = dot_t(kept, s_kept) + dot_t(i2, s_second) + dot_t(i3, s_third)
        outs.append(sc.astype(BF16).reshape(8, r, 2, 256).transpose(2, 0, 1, 3))
    sc = jnp.stack(outs, axis=2)
    sc = jnp.where(k == 0, sc, sc[::-1]).reshape(16, 64, 256)
    sc = lax.all_to_all(sc, ("core", "x", "zl"), 0, 0, tiled=True)
    return sc.reshape(2, 8, 64, 256).astype(F32).sum(axis=1).astype(BF16).reshape(128, 256)


def solution(mesh):
    fine = Mesh(mesh.devices.reshape(4, 4, 2, 4, 2), AXES)
    rows, cols = ("zh", "y", "core"), ("x", "zl")
    return jax.shard_map(
        local,
        mesh=fine,
        in_specs=(P(None, rows), P(rows, cols), P(rows, cols)),
        out_specs=P(cols, rows),
        check_vma=False,
    )
```

```python
import jax
import jax.numpy as jnp
from jax import lax
from jax.sharding import Mesh, PartitionSpec as P

F32, BF16 = jnp.float32, jnp.bfloat16
AXES = ("zh", "y", "core", "x", "zl")
CHUNKS = 2
SWAP = [(0, 1), (1, 0)]
NEAR = [(0, 1), (1, 0), (2, 3), (3, 2)]
WRAP = [(0, 3), (3, 0), (1, 2), (2, 1)]


def by_core(first, second):
    return [(2 * s, 2 * d) for s, d in first] + [(2 * s + 1, 2 * d + 1) for s, d in second]


STEP1, STEP2 = by_core(NEAR, WRAP), by_core(WRAP, NEAR)


def dot(a, b):
    return jnp.dot(a, b, preferred_element_type=F32)


def dot_t(a, b):
    return lax.dot_general(a, b, (((1,), (1,)), ((), ())), preferred_element_type=F32)


def cut(a, i, size):
    return lax.dynamic_slice_in_dim(a, i * size, size, 1)


def local(queries, gram, slab):
    y, k = lax.axis_index("y"), lax.axis_index("core")
    p = jnp.where(k == 0, ((y + 1) // 2) % 2, y // 2)
    s = jnp.where(k == 0, y // 2, y % 2)
    t = jnp.where(k == 0, s, 1 - s)
    n = 512 // CHUNKS
    r = 64 // CHUNKS

    g_in = lax.ppermute(gram, "core", SWAP)
    rows = queries.reshape(8, 2, CHUNKS, r, 512)

    def for_core(core):
        picked = lax.dynamic_index_in_dim(rows, core, 1, keepdims=False)
        return picked.transpose(1, 0, 2, 3).reshape(CHUNKS, n, 512)

    q_mine = for_core(k)
    q_in = lax.ppermute(for_core(1 - k), "core", SWAP)
    s_in = lax.ppermute(slab, "core", SWAP)
    both = jnp.concatenate([slab, s_in])
    s_kept = cut(both, p, 1024)
    s_second, s_third = cut(both, 2 * (1 - p) + t, 512), cut(both, 2 * (1 - p) + 1 - t, 512)
    outs = []
    for c in range(CHUNKS):
        part = dot(q_mine[c], gram) + dot(q_in[c], g_in)
        got = lax.ppermute(cut(part, 1 - p, 1024).astype(BF16), ("y", "core"), STEP1)
        part = cut(part, p, 1024) + got.astype(F32)
        second = cut(part, 1 - s, 512).astype(BF16)
        got = lax.ppermute(second, ("y", "core"), STEP2)
        piece = cut(part, s, 512) + got.astype(F32)
        piece = piece + lax.ppermute(piece.astype(BF16), ("zh", "core"), STEP1).astype(F32)
        piece = piece + lax.ppermute(piece.astype(BF16), ("zh", "core"), STEP2).astype(F32)
        i0 = piece.astype(BF16)
        i1 = lax.ppermute(i0, ("y", "core"), STEP2)
        kept = jnp.where(s == 0, jnp.concatenate([i0, i1], axis=1), jnp.concatenate([i1, i0], axis=1))
        if c < CHUNKS - 1:
            i23 = lax.ppermute(jnp.concatenate([i0, i1], axis=1), ("y", "core"), STEP1)
            i2, i3 = i23[:, :512], i23[:, 512:]
        else:
            i2 = lax.ppermute(i0, ("y", "core"), STEP1)
            i3 = lax.ppermute(i1, ("y", "core"), STEP1)
        sc = dot_t(kept, s_kept) + dot_t(i2, s_second) + dot_t(i3, s_third)
        outs.append(sc.astype(BF16).reshape(8, r, 2, 256).transpose(2, 0, 1, 3))
    sc = jnp.stack(outs, axis=2)
    sc = jnp.where(k == 0, sc, sc[::-1]).reshape(16, 64, 256)
    sc = lax.all_to_all(sc, ("core", "x", "zl"), 0, 0, tiled=True)
    return sc.reshape(2, 8, 64, 256).astype(F32).sum(axis=1).astype(BF16).reshape(128, 256)


def solution(mesh):
    fine = Mesh(mesh.devices.reshape(4, 4, 2, 4, 2), AXES)
    rows, cols = ("zh", "y", "core"), ("x", "zl")
    return jax.shard_map(
        local,
        mesh=fine,
        in_specs=(P(None, rows), P(rows, cols), P(rows, cols)),
        out_specs=P(cols, rows),
        check_vma=False,
    )
```

```python
import jax
import jax.numpy as jnp
from jax import lax
from jax.sharding import Mesh, PartitionSpec as P

F32, BF16 = jnp.float32, jnp.bfloat16
AXES = ("zh", "y", "core", "x", "zl")
CHUNKS = 2
SWAP = [(0, 1), (1, 0)]
NEAR = [(0, 1), (1, 0), (2, 3), (3, 2)]
WRAP = [(0, 3), (3, 0), (1, 2), (2, 1)]


def by_core(first, second):
    return [(2 * s, 2 * d) for s, d in first] + [(2 * s + 1, 2 * d + 1) for s, d in second]


STEP1, STEP2 = by_core(NEAR, WRAP), by_core(WRAP, NEAR)


def dot(a, b):
    return jnp.dot(a, b, preferred_element_type=F32)


def dot_t(a, b):
    return lax.dot_general(a, b, (((1,), (1,)), ((), ())), preferred_element_type=F32)


def cut(a, i, size):
    return lax.dynamic_slice_in_dim(a, i * size, size, 1)


def local(queries, gram, slab):
    y, k = lax.axis_index("y"), lax.axis_index("core")
    p = jnp.where(k == 0, ((y + 1) // 2) % 2, y // 2)
    s = jnp.where(k == 0, y // 2, y % 2)
    t = jnp.where(k == 0, s, 1 - s)
    n = 512 // CHUNKS
    r = 64 // CHUNKS

    g_in = lax.ppermute(gram, "core", SWAP)
    rows = queries.reshape(8, 2, CHUNKS, r, 512)

    def for_core(core):
        picked = lax.dynamic_index_in_dim(rows, core, 1, keepdims=False)
        return picked.transpose(1, 0, 2, 3).reshape(CHUNKS, n, 512)

    q_mine = for_core(k)
    q_in = lax.ppermute(for_core(1 - k), "core", SWAP)
    s_in = lax.ppermute(slab, "core", SWAP)
    both = jnp.concatenate([slab, s_in])
    s_kept = cut(both, p, 1024)
    s_second, s_third = cut(both, 2 * (1 - p) + t, 512), cut(both, 2 * (1 - p) + 1 - t, 512)
    outs = []
    for c in range(CHUNKS):
        part = dot(q_mine[c], gram) + dot(q_in[c], g_in)
        got = lax.ppermute(cut(part, 1 - p, 1024).astype(BF16), ("y", "core"), STEP1)
        part = cut(part, p, 1024) + got.astype(F32)
        second = cut(part, 1 - s, 512).astype(BF16)
        got = lax.ppermute(second, ("y", "core"), STEP2)
        piece = cut(part, s, 512) + got.astype(F32)
        piece = piece + lax.ppermute(piece.astype(BF16), ("zh", "core"), STEP1).astype(F32)
        piece = piece + lax.ppermute(piece.astype(BF16), ("zh", "core"), STEP2).astype(F32)
        i0 = piece.astype(BF16)
        i1 = lax.ppermute(i0, ("y", "core"), STEP2)
        kept = jnp.where(s == 0, jnp.concatenate([i0, i1], axis=1), jnp.concatenate([i1, i0], axis=1))
        i2 = lax.ppermute(i0, ("y", "core"), STEP1)
        i3 = lax.ppermute(i1, ("y", "core"), STEP1)
        sc = dot_t(i3, s_third) + (dot_t(i2, s_second) + dot_t(kept, s_kept))
        outs.append(sc.astype(BF16).reshape(8, r, 2, 256).transpose(2, 0, 1, 3))
    sc = jnp.stack(outs, axis=2)
    sc = jnp.where(k == 0, sc, sc[::-1]).reshape(16, 64, 256)
    sc = lax.all_to_all(sc, ("core", "x", "zl"), 0, 0, tiled=True)
    return sc.reshape(2, 8, 64, 256).astype(F32).sum(axis=1).astype(BF16).reshape(128, 256)


def solution(mesh):
    fine = Mesh(mesh.devices.reshape(4, 4, 2, 4, 2), AXES)
    rows, cols = ("zh", "y", "core"), ("x", "zl")
    return jax.shard_map(
        local,
        mesh=fine,
        in_specs=(P(None, rows), P(rows, cols), P(rows, cols)),
        out_specs=P(cols, rows),
        check_vma=False,
    )
```
